512 devices in a mesh: req: 32 (over y, x, core), tp: 16 (over z).
Axes of the slice: x: 4, y: 4, z: 16, core: 2. Of those that a mesh axis runs over, the one named last changes fastest.
Arguments:
- queries: bfloat16 [32, 512, 16384], P('req', None, 'tp'), may hold values from -400 to 400
- kv_heads: bfloat16 [32, 16, 512, 128], P('req', None, 'tp'), may hold values from -100 to 100
- bit_widths: int32 [16], P('tp'), may hold values from 2 to 8, as said below
- destinations: int32 [32, 32, 1], P('req'), may hold values from 0 to 31; in each aligned block of 32 rows (0 to 31, 32 to 63, ..., all dimensions but the last counted through in order) at most 2 rows name the same one
- lengths: int32 [32], P('req'), may hold values from 128 to 512, as said below
Outputs:
- rotated: bfloat16 [32, 512, 16384], P('req', None, 'tp')
- page_codes: bfloat16 [32, 32, 2, 16, 16, 128], P('req', None, None, 'tp')
- page_steps: bfloat16 [32, 32, 2, 16], P('req', None, None, 'tp')
The draws below stay inside these ranges and needn't reach their ends.
Inputs may be any that keep to these rules, and one draw needn't show every extreme that they name: `destinations`: no owner is named more than 2 times among one group's pages. `bit_widths`: each entry is 2, 4 or 8. `lengths`: some group has all 512 tokens valid.
All inputs are finite; a program needn't handle non-finite values.
Results may differ from the reference program's by a relative error of at most 0.012.
Values may be sent and summed in bfloat16 or wider, within the bound.
No kernel may reach another device: no remote copies, remote signals or barrier semaphores. Data moves between devices by JAX's collectives and lax.ppermute only.
A program may use at most 64 MiB of HBM per device.

```python
import math
import jax
import jax.numpy as jnp
import numpy as np
from jax import lax

QH = 128
KVH = 8
HD = 128
L = 512
PAGE = 16
GROUPS = 32
OWNERS = 32
PAGES = 32
CAP = 2
N_REQ = 32


def attention_pair(key, spread):
    base = jax.random.fold_in(key, 7)
    row_scale = jnp.exp(jax.random.uniform(jax.random.fold_in(base, 1), (GROUPS, 2 * KVH, L, 1), minval=-spread, maxval=spread))
    col_scale = jnp.exp(jax.random.uniform(jax.random.fold_in(base, 2), (GROUPS, 2 * KVH, 1, HD), minval=-math.log(3.0), maxval=math.log(3.0)))
    kv_rows = jnp.clip(jax.random.normal(jax.random.fold_in(base, 3), (GROUPS, 2 * KVH, L, HD)), -6.0, 6.0) * row_scale * col_scale
    query_rows = jnp.clip(jax.random.normal(jax.random.fold_in(base, 4), (GROUPS, L, QH, HD)), -6.0, 6.0)
    group_size = QH // KVH
    marks = jnp.arange(4, dtype=jnp.int32)
    kv_head = (jax.random.randint(jax.random.fold_in(base, 5), (GROUPS, 1), 0, KVH) + 2 * marks[None, :]) % KVH
    query_head = kv_head * group_size + jax.random.randint(jax.random.fold_in(base, 6), (GROUPS, 4), 0, group_size)
    first_key = marks[None, :] * (L // 32) + jax.random.randint(jax.random.fold_in(base, 8), (GROUPS, 4), 0, L // 64)
    second_key = first_key + L // 64
    query_place = L // 8 + marks[None, :] * (L // 32) + jax.random.randint(jax.random.fold_in(base, 9), (GROUPS, 4), 0, L // 32)
    group_ids = jnp.arange(GROUPS, dtype=jnp.int32)[:, None]
    key_row = 2 * kv_head
    kv_rows = kv_rows.at[group_ids, key_row, first_key].set(kv_rows[group_ids, key_row, first_key])
    kv_rows = kv_rows.at[group_ids, key_row, second_key].set(kv_rows[group_ids, key_row, second_key])
    query_rows = query_rows.at[group_ids, query_place, query_head].set(query_rows[group_ids, query_place, query_head])
    return (query_rows.reshape(GROUPS, L, QH * HD), kv_rows)


def draw_queries(key, part):
    both = attention_pair(key, math.log(3.0))
    return both[0].astype(jnp.bfloat16)


def draw_kv_heads(key, part):
    both = attention_pair(key, math.log(3.0))
    return both[1].astype(jnp.bfloat16)


def draw_bit_widths(key, part):
    key = jax.random.fold_in(key, 21)
    picks = jax.random.randint(jax.random.fold_in(key, 1), (2 * KVH,), 0, 3)
    widths = jnp.array([2, 4, 8], jnp.int32)[picks]
    first_spot = jax.random.randint(jax.random.fold_in(key, 2), (), 0, 2 * KVH)
    second_spot = (first_spot + 1 + jax.random.randint(jax.random.fold_in(key, 3), (), 0, 2 * KVH - 1)) % (2 * KVH)
    widths = widths.at[first_spot].set(8)
    widths = widths.at[second_spot].set(2)
    return widths.astype(jnp.int32)


def draw_lengths(key, part):
    key = jax.random.fold_in(key, 31)
    counts = jax.random.randint(jax.random.fold_in(key, 1), (GROUPS,), L // 4, L + 1)
    full_spot = jax.random.randint(jax.random.fold_in(key, 2), (), 0, GROUPS)
    counts = counts.at[full_spot].set(L)
    return counts.astype(jnp.int32)


def routed_block(rng, own, number, rows, count, top, bound, lean):
    ranking = jax.random.permutation(rng, count)
    heavy_load, usual = load_shares(count, rows * top, bound, lean, True), load_shares(count, rows * top, bound, lean, False)
    places = jnp.arange(count)

    def named(sizes, rotation):
        used = int((sizes > 0).sum())
        fixed = max(1, used // 4)
        moved = fixed + (places - fixed + rotation * (used - fixed)) % max(1, count - fixed)
        return jnp.zeros((count,), jnp.int32).at[ranking[jnp.where(places < fixed, places, moved)]].set(jnp.asarray(sizes, jnp.int32))

    sizes = jnp.where(number % 4 == 0, named(heavy_load, number // 4), named(usual, number - number // 4 - 1))
    mixed = jax.random.permutation(jax.random.fold_in(own, 3), count)
    donor, taker = mixed[0:count // 2 * 2:2], mixed[1:count // 2 * 2:2]
    margin = jnp.minimum(sizes[donor] - 1, bound - sizes[taker]) // 2
    margin = jnp.where((donor == ranking[0]) | (taker == ranking[0]) | (sizes[taker] == 0), 0, jnp.maximum(margin, 0))
    moved = jax.random.randint(jax.random.fold_in(own, 4), (count // 2,), 0, 1 << 20) % (margin + 1)
    sizes = sizes.at[donor].add(-moved).at[taker].add(moved)
    items = jnp.searchsorted(jnp.cumsum(sizes), jnp.arange(rows * top), side="right").astype(jnp.int32)
    grid = items.reshape(top, rows).T
    grid = grid[jax.random.permutation(jax.random.fold_in(own, 1), rows)]
    rotation = jax.random.randint(jax.random.fold_in(own, 2), (rows, 1), 0, top)
    return jnp.take_along_axis(grid, (jnp.arange(top)[None, :] + rotation) % top, axis=1)


def load_shares(count, total, limit, slope, full):
    loads = [(1 << 20) // math.isqrt(grade ** slope) + 1 for grade in range(1, count + 1)]
    largest = limit if full else min(limit, max(-(-total // count), total * loads[0] // sum(loads)))
    least = 1 if total - largest >= count - 1 else 0
    given, rest = [largest] + [least] * (count - 1), total - largest - least * (count - 1)
    while rest > 0:
        movable = [i for i in range(1, count) if given[i] < largest] or [i for i in range(1, count) if given[i] < limit]
        mass, remaining = sum([loads[i] for i in movable]), rest
        for i in movable:
            more = min(limit - given[i], max(1, remaining * loads[i] // mass), rest)
            given[i] = given[i] + more
            rest = rest - more
    return np.array(given)


def setup_inputs(seed: int = 0) -> dict:
    seeds = jax.random.split(jax.random.key(seed), 6)
    queries = draw_queries(jax.random.fold_in(seeds[5], 71), 0)
    kv_heads = draw_kv_heads(jax.random.fold_in(seeds[5], 71), 0)
    bit_widths = draw_bit_widths(jax.random.fold_in(seeds[5], 71), 0)
    destinations_keys = jax.random.split(jax.random.fold_in(seeds[3], 1), GROUPS * PAGES // PAGES)
    destinations_turns = jax.random.permutation(jax.random.fold_in(seeds[3], 3), GROUPS * PAGES // PAGES)
    destinations = jax.vmap(lambda own, number: routed_block(jax.random.fold_in(seeds[3], 2), own, number, PAGES, N_REQ, 1, CAP, 2))(destinations_keys, destinations_turns).reshape((GROUPS, PAGES, 1))
    lengths = draw_lengths(jax.random.fold_in(seeds[5], 71), 0)
    return dict(queries=queries, kv_heads=kv_heads, bit_widths=bit_widths, destinations=destinations, lengths=lengths)


def butterfly(values_now, bit_index):
    shape_now = values_now.shape
    stride = 1 << bit_index
    halves = values_now.reshape(shape_now[:-2] + (shape_now[-2] // (2 * stride), 2, stride, shape_now[-1])).astype(jnp.float32)
    low_half = halves[..., 0, :, :]
    high_half = halves[..., 1, :, :]
    factor = math.sqrt(0.5)
    joined = jnp.stack([(low_half + high_half) * factor, (low_half - high_half) * factor], axis=-3)
    return joined.reshape(shape_now).astype(jnp.bfloat16)

def attend_group(pieces):
    query_block, kv_block, length = pieces
    group_size = QH // KVH
    places = jnp.arange(L)
    query_heads = query_block.reshape(L, KVH, group_size, HD).transpose(1, 0, 2, 3).astype(jnp.float32)
    key_rows = kv_block[0::2].astype(jnp.float32)
    value_rows = kv_block[1::2].astype(jnp.float32)
    causal = places[:, None] >= places[None, :]

    def one_head(items):
        query_part, key_part, value_part = items
        scores = jnp.einsum('qgd,kd->gqk', query_part, key_part) / math.sqrt(HD)
        scores = jnp.where(causal, scores, -jnp.inf)
        shifted = jnp.exp(scores - lax.optimization_barrier(jnp.max(scores, axis=-1, keepdims=True)))
        weights = (shifted / lax.optimization_barrier(jnp.sum(shifted, axis=-1, keepdims=True))).astype(jnp.bfloat16)
        return jnp.einsum('gqk,kd->qgd', weights.astype(jnp.float32), value_part)
    attended = lax.map(one_head, (query_heads, key_rows, value_rows))
    attended = jnp.where((places < length)[None, :, None, None], attended, 0.0).astype(jnp.bfloat16)
    return attended.transpose(1, 0, 2, 3).reshape(L, QH * HD)

def reference(queries, kv_heads, bit_widths, destinations, lengths):
    attended = lax.map(attend_group, (queries, kv_heads, lengths))
    rotated = attended.reshape(GROUPS, L, QH, HD)
    for bit_index in range(QH.bit_length() - 1):
        rotated = butterfly(rotated, bit_index)
    rotated = rotated.reshape(GROUPS, L, QH * HD)
    places = jnp.arange(L)
    zero_value = jnp.zeros((), jnp.bfloat16)
    live_rows = jnp.where(places[None, None, :, None] < lengths[:, None, None, None], kv_heads, zero_value)
    page_rows = live_rows.reshape(GROUPS, 2 * KVH, PAGES, PAGE, HD).astype(jnp.float32)
    page_rms = jnp.sqrt(lax.optimization_barrier(jnp.mean(page_rows * page_rows, axis=(3, 4))) + 1e-06)
    page_step = (page_rms * 0.5).astype(jnp.bfloat16)
    levels = (2 ** (bit_widths - 1) - 1).astype(jnp.float32)[None, :, None, None, None]
    code_values = jnp.clip(page_rows / page_step.astype(jnp.float32)[..., None, None], -levels, levels).astype(jnp.bfloat16)
    owner_of = destinations[:, :, 0]
    owner_ids = jnp.arange(OWNERS, dtype=jnp.int32)
    chosen = (owner_of[:, :, None] == owner_ids[None, None, :]).astype(jnp.int32)
    earlier = jnp.cumsum(chosen, axis=1) - chosen
    slot_of = lax.optimization_barrier(jnp.sum(earlier * chosen, axis=2))
    slot_ids = jnp.arange(CAP, dtype=jnp.int32)
    select = ((owner_of[:, None, None, :] == owner_ids[None, :, None, None]) & (slot_of[:, None, None, :] == slot_ids[None, None, :, None])).astype(jnp.int32)
    page_ids = jnp.arange(PAGES, dtype=jnp.int32)
    which_page = lax.optimization_barrier(jnp.sum(select * page_ids[None, None, None, :], axis=3)).astype(jnp.int32)
    filled = lax.optimization_barrier(jnp.sum(select, axis=3)) > 0
    group_ids = jnp.arange(GROUPS, dtype=jnp.int32)[:, None, None]
    by_page = code_values.transpose(0, 2, 1, 3, 4)
    picked = by_page[group_ids, which_page]
    picked = jnp.where(filled[..., None, None, None], picked, zero_value)
    page_codes = picked.transpose(1, 0, 2, 3, 4, 5)
    step_pick = page_step.transpose(0, 2, 1)[group_ids, which_page]
    step_pick = jnp.where(filled[..., None], step_pick, zero_value)
    page_steps = step_pick.transpose(1, 0, 2, 3)
    return (rotated, page_codes, page_steps)
```

```python
import math

import jax
import jax.numpy as jnp
from jax import lax
from jax.sharding import PartitionSpec as P

PAGE = 16


def sign_matrix(count):
    row = lax.broadcasted_iota(jnp.int32, (count, count), 0)
    col = lax.broadcasted_iota(jnp.int32, (count, count), 1)
    both = row & col
    parity = jnp.zeros_like(both)
    for bit in range(count.bit_length() - 1):
        parity = parity ^ (jnp.right_shift(both, bit) & 1)
    return (1 - 2 * parity).astype(jnp.bfloat16)


def attend_local(query_block, key_rows, value_rows, length, heads):
    seq_len, head_dim = key_rows.shape
    query_heads = query_block.reshape(seq_len, heads, head_dim)
    block_rows = min(256, seq_len)
    places = jnp.arange(seq_len)
    outputs = []
    for first_row in range(0, seq_len, block_rows):
        finish = first_row + block_rows
        scores = jnp.einsum(
            "qgd,kd->gqk",
            query_heads[first_row:finish],
            key_rows[:finish],
            preferred_element_type=jnp.float32,
        ) / math.sqrt(head_dim)
        causal = (first_row + jnp.arange(block_rows))[:, None] >= jnp.arange(finish)[None, :]
        scores = jnp.where(causal, scores, -jnp.inf)
        shifted = jnp.exp(scores - jnp.max(scores, axis=-1, keepdims=True))
        weights = (shifted / jnp.sum(shifted, axis=-1, keepdims=True)).astype(jnp.bfloat16)
        outputs.append(
            jnp.einsum(
                "gqk,kd->gqd",
                weights,
                value_rows[:finish],
                preferred_element_type=jnp.float32,
            )
        )
    attended = jnp.concatenate(outputs, axis=1)
    return jnp.where((places < length)[None, :, None], attended, 0.0).astype(jnp.bfloat16)


def body(queries, kv_heads, bit_widths, destinations, lengths):
    length = lengths[0]
    local_kv = kv_heads[0]
    total_rows, tok_here, head_dim = local_kv.shape
    tp_count = lax.axis_size("tp")
    rows_here = total_rows // tp_count
    paired = local_kv.reshape(total_rows // 2, 2, tok_here, head_dim)
    outgoing = jnp.repeat(paired, tp_count // (total_rows // 2), axis=0)
    received = lax.all_to_all(outgoing, "tp", split_axis=0, concat_axis=2, tiled=True)[0]
    seq_len = received.shape[1]
    own_rows = lax.dynamic_slice_in_dim(received, lax.axis_index("tp") % 2, 1, 0)
    heads_here = queries.shape[2] // head_dim
    attended = attend_local(queries[0], received[0], received[1], length, heads_here)

    share = seq_len // tp_count
    blocks = attended.reshape(heads_here, tp_count, share, head_dim).transpose(1, 0, 2, 3)
    blocks = lax.all_to_all(blocks, "tp", split_axis=0, concat_axis=0, tiled=True)
    all_heads = tp_count * heads_here
    mixed = jnp.dot(
        sign_matrix(all_heads),
        blocks.reshape(all_heads, share * head_dim),
        preferred_element_type=jnp.float32,
    ) * (1.0 / math.sqrt(all_heads))
    mixed = mixed.astype(jnp.bfloat16).reshape(tp_count, heads_here, share, head_dim)
    back = lax.all_to_all(mixed, "tp", split_axis=0, concat_axis=0, tiled=True)
    rotated = back.transpose(0, 2, 1, 3).reshape(1, seq_len, heads_here * head_dim)

    pages_count = seq_len // PAGE
    owners = lax.axis_size("req")
    capacity = max(2, (3 * pages_count + 2 * owners - 1) // (2 * owners))
    places = jnp.arange(seq_len)
    live_rows = jnp.where(places[None, :, None] < length, own_rows, jnp.zeros((), jnp.bfloat16))
    page_rows = live_rows.reshape(rows_here, pages_count, PAGE, head_dim).astype(jnp.float32)
    page_rms = jnp.sqrt(jnp.mean(page_rows * page_rows, axis=(2, 3)) + 1e-06)
    page_step = (page_rms * 0.5).astype(jnp.bfloat16)
    levels = (2 ** (bit_widths - 1) - 1).astype(jnp.float32)[:, None, None, None]
    code_values = jnp.clip(
        page_rows / page_step.astype(jnp.float32)[:, :, None, None], -levels, levels
    ).astype(jnp.bfloat16)
    owner_of = destinations[0, :, 0]
    owner_ids = jnp.arange(owners, dtype=jnp.int32)
    chosen = (owner_of[:, None] == owner_ids[None, :]).astype(jnp.int32)
    earlier = jnp.cumsum(chosen, axis=0) - chosen
    slot_of = jnp.sum(earlier * chosen, axis=1)
    slot_ids = jnp.arange(capacity, dtype=jnp.int32)
    select = (
        (owner_of[None, None, :] == owner_ids[:, None, None])
        & (slot_of[None, None, :] == slot_ids[None, :, None])
    ).astype(jnp.bfloat16)
    select = select.reshape(owners * capacity, pages_count)
    width = rows_here * PAGE * head_dim
    flat_codes = code_values.transpose(1, 0, 2, 3).reshape(pages_count, width)
    steps_wide = jnp.broadcast_to(page_step.T[:, :, None], (pages_count, rows_here, head_dim))
    flat = jnp.concatenate([flat_codes, steps_wide.reshape(pages_count, -1)], axis=1)
    packed = jnp.dot(select, flat, preferred_element_type=jnp.float32).astype(jnp.bfloat16)
    packed = packed.reshape(owners, capacity, -1)
    got = lax.all_to_all(packed, "req", split_axis=0, concat_axis=0, tiled=True)
    got_codes = got[:, :, :width].reshape(owners, capacity, rows_here, PAGE, head_dim)
    got_steps = got[:, :, width:].reshape(owners, capacity, rows_here, head_dim)[..., 0]
    return (rotated, got_codes[None], got_steps[None])


def solution(mesh):
    in_specs = (
        P("req", None, "tp"),
        P("req", None, "tp", None),
        P("tp"),
        P("req", None, None),
        P("req"),
    )
    out_specs = (
        P("req", None, "tp"),
        P("req", None, None, "tp", None, None),
        P("req", None, None, "tp"),
    )
    return jax.shard_map(body, mesh=mesh, in_specs=in_specs, out_specs=out_specs, check_vma=False)
```

```python
import functools
import math

import jax
import jax.numpy as jnp
from jax import lax
from jax.experimental import pallas as pl
from jax.experimental.pallas import tpu as pltpu
from jax.sharding import PartitionSpec as P

PAGE = 16
BLOCK = 128


def attend_kernel(length_ref, q_ref, kv_ref, out_ref, k_ref, v_ref, *, blocks, heads):
    head_dim = k_ref.shape[1]
    seq_len = k_ref.shape[0]
    step = pl.program_id(0)

    @pl.when(step == 0)
    def _():
        k_ref[...] = kv_ref[:, 0].reshape(seq_len, head_dim)
        v_ref[:, :head_dim] = kv_ref[:, 1].reshape(seq_len, head_dim)
        v_ref[:, head_dim:] = jnp.ones((seq_len, head_dim), jnp.bfloat16)

    rate = math.log2(math.e) / math.sqrt(head_dim)
    rows = lax.broadcasted_iota(jnp.int32, (BLOCK, BLOCK), 0)
    cols = lax.broadcasted_iota(jnp.int32, (BLOCK, BLOCK), 1)
    causal = rows >= cols
    live = step * BLOCK + lax.broadcasted_iota(jnp.int32, (BLOCK, head_dim), 0) < length_ref[0]

    def attend(index):
        finish = (index + 1) * BLOCK
        for head in range(heads):
            columns = slice(head * head_dim, (head + 1) * head_dim)
            scores = lax.dot_general(
                q_ref[:, columns],
                k_ref[:finish],
                (((1,), (1,)), ((), ())),
                preferred_element_type=jnp.float32,
            )
            last = jnp.where(causal, scores[:, index * BLOCK :], -jnp.inf)
            if index:
                scores = jnp.concatenate([scores[:, : index * BLOCK], last], axis=1)
            else:
                scores = last
            top = jnp.max(scores, axis=1, keepdims=True)
            weights = jnp.exp2((scores - top) * rate).astype(jnp.bfloat16)
            both = jnp.dot(weights, v_ref[:finish], preferred_element_type=jnp.float32)
            attended = both[:, :head_dim] / both[:, head_dim:]
            out_ref[:, columns] = jnp.where(live, attended, 0.0).astype(jnp.bfloat16)

    for index in range(blocks):
        pl.when(step == index)(functools.partial(attend, index))


def attend_local(queries, received, length, head_dim):
    seq_len, width = queries.shape
    heads = width // head_dim
    blocks = seq_len // BLOCK
    return pl.pallas_call(
        functools.partial(attend_kernel, blocks=blocks, heads=heads),
        grid=(blocks,),
        in_specs=[
            pl.BlockSpec(memory_space=pltpu.SMEM),
            pl.BlockSpec((BLOCK, width), lambda i: (i, 0)),
            pl.BlockSpec(received.shape, lambda i: (0, 0, 0, 0)),
        ],
        out_specs=pl.BlockSpec((BLOCK, width), lambda i: (i, 0)),
        out_shape=jax.ShapeDtypeStruct((seq_len, width), jnp.bfloat16),
        scratch_shapes=[
            pltpu.VMEM((seq_len, head_dim), jnp.bfloat16),
            pltpu.VMEM((seq_len, 2 * head_dim), jnp.bfloat16),
        ],
        compiler_params=pltpu.CompilerParams(vmem_limit_bytes=32 * 1024 * 1024),
        cost_estimate=pl.CostEstimate(
            flops=4 * seq_len * seq_len * width,
            bytes_accessed=4 * seq_len * width,
            transcendentals=seq_len * seq_len * heads,
        ),
        name="attend",
    )(length, queries, received)


def butterflies(values):
    values = list(values)
    stride = 1
    while stride < len(values):
        for low in range(len(values)):
            if not low & stride:
                a, b = values[low], values[low + stride]
                values[low], values[low + stride] = a + b, a - b
        stride *= 2
    return values


def hadamard_kernel(in_ref, out_ref, mid_ref, *, heads):
    devices, tokens, width = in_ref.shape
    head_dim = width // heads
    factor = 1.0 / math.sqrt(devices * heads)
    columns = [slice(h * head_dim, (h + 1) * head_dim) for h in range(heads)]
    for first in range(0, tokens, PAGE):
        rows = slice(first, first + PAGE)
        for device in range(devices):
            tiles = butterflies([in_ref[device, rows, c].astype(jnp.float32) for c in columns])
            for c, tile in zip(columns, tiles):
                mid_ref[device, :, c] = tile
        for c in columns:
            tiles = butterflies([mid_ref[device, :, c] for device in range(devices)])
            for device, tile in enumerate(tiles):
                out_ref[device, rows, c] = (tile * factor).astype(jnp.bfloat16)


def hadamard(blocks, heads):
    devices, tokens, width = blocks.shape
    spec = pl.BlockSpec((devices, PAGE, width), lambda i: (0, i, 0))
    return pl.pallas_call(
        functools.partial(hadamard_kernel, heads=heads),
        grid=(tokens // PAGE,),
        in_specs=[spec],
        out_specs=spec,
        out_shape=jax.ShapeDtypeStruct(blocks.shape, jnp.bfloat16),
        scratch_shapes=[pltpu.VMEM((devices, PAGE, width), jnp.float32)],
        compiler_params=pltpu.CompilerParams(vmem_limit_bytes=32 * 1024 * 1024),
        cost_estimate=pl.CostEstimate(
            flops=7 * blocks.size, bytes_accessed=4 * blocks.size, transcendentals=0
        ),
        name="hadamard",
    )(blocks)


def pick_kernel(which_ref, filled_ref, every_ref, out_ref, sems, *, capacity):
    count = out_ref.shape[0]

    def copy(item):
        first = pl.multiple_of(which_ref[item] * PAGE, PAGE)
        return pltpu.make_async_copy(
            every_ref.at[item // capacity, pl.ds(first, PAGE)], out_ref.at[item], sems.at[item]
        )

    for item in range(count):
        copy(item).start()
    for item in range(count):
        copy(item).wait()
        page = out_ref[item]
        out_ref[item] = jnp.where(filled_ref[item] > 0, page, jnp.zeros_like(page))


def pick_pages(every, which, filled, capacity):
    count = which.shape[0]
    head_dim = every.shape[2]
    smem = pl.BlockSpec(memory_space=pltpu.SMEM)
    return pl.pallas_call(
        functools.partial(pick_kernel, capacity=capacity),
        in_specs=[smem, smem, pl.BlockSpec(memory_space=pl.ANY)],
        out_specs=pl.BlockSpec(memory_space=pltpu.VMEM),
        out_shape=jax.ShapeDtypeStruct((count, PAGE, head_dim), jnp.bfloat16),
        scratch_shapes=[pltpu.SemaphoreType.DMA((count,))],
        cost_estimate=pl.CostEstimate(
            flops=0, bytes_accessed=4 * count * PAGE * head_dim, transcendentals=0
        ),
        name="pick_pages",
    )(which, filled, every)


def page_parts(own_rows, bit_widths, owner_of, length):
    seq_len, head_dim = own_rows.shape
    pages = seq_len // PAGE
    places = jnp.arange(seq_len)
    live_rows = jnp.where(places[:, None] < length, own_rows, jnp.zeros((), jnp.bfloat16))
    page_rows = live_rows.reshape(pages, PAGE, head_dim).astype(jnp.float32)
    page_rms = jnp.sqrt(jnp.mean(page_rows * page_rows, axis=(1, 2)) + 1e-06)
    page_step = (page_rms * 0.5).astype(jnp.bfloat16)
    level = (2 ** (bit_widths[0] - 1) - 1).astype(jnp.float32)
    codes = jnp.clip(page_rows / page_step.astype(jnp.float32)[:, None, None], -level, level)
    page_ids = jnp.arange(pages)
    same = (owner_of[:, None] == owner_of[None, :]) & (page_ids[None, :] < page_ids[:, None])
    slot_of = jnp.sum(same.astype(jnp.int32), axis=1)
    return codes.astype(jnp.bfloat16), page_step, slot_of


def body(queries, kv_heads, bit_widths, destinations, lengths):
    length = lengths[0]
    local_kv = kv_heads[0]
    total_rows, tok_here, head_dim = local_kv.shape
    tp_count = lax.axis_size("tp")
    owners = lax.axis_size("req")
    paired = local_kv.reshape(total_rows // 2, 2, tok_here, head_dim)
    outgoing = jnp.repeat(paired, tp_count // (total_rows // 2), axis=0)
    received = lax.all_to_all(outgoing, "tp", split_axis=0, concat_axis=0, tiled=True)
    seq_len = tp_count * tok_here
    heads_here = queries.shape[2] // head_dim

    attended = attend_local(queries[0], received, lengths, head_dim)
    blocks = attended.reshape(tp_count, seq_len // tp_count, heads_here * head_dim)
    blocks = lax.all_to_all(blocks, "tp", split_axis=0, concat_axis=0, tiled=True)
    mixed = hadamard(blocks, heads_here)
    back = lax.all_to_all(mixed, "tp", split_axis=0, concat_axis=0, tiled=True)
    rotated = back.reshape(1, seq_len, heads_here * head_dim)

    pages = seq_len // PAGE
    capacity = max(2, (3 * pages + 2 * owners - 1) // (2 * owners))
    own_rows = lax.dynamic_index_in_dim(received, lax.axis_index("tp") % 2, 1, keepdims=False)
    own_rows = own_rows.reshape(seq_len, head_dim)
    codes, steps, slots = page_parts(own_rows, bit_widths, destinations[0, :, 0], length)
    target = destinations[0, :, 0] * capacity + slots
    extra = jnp.broadcast_to(
        jnp.stack([steps, target.astype(jnp.bfloat16)])[:, :, None], (2, pages, head_dim)
    )
    sent = jnp.concatenate([codes.reshape(seq_len, head_dim), extra.reshape(2 * pages, head_dim)])
    every = lax.all_gather(sent, "req", axis=0, tiled=False)
    every_steps = every[:, seq_len : seq_len + pages, 0]
    every_target = every[:, seq_len + pages :, 0].astype(jnp.int32)
    mine = lax.axis_index("req") * capacity + jnp.arange(capacity)
    select = (every_target[:, None, :] == mine[None, :, None]).astype(jnp.int32)
    which = jnp.sum(select * jnp.arange(pages), axis=2).reshape(owners * capacity)
    filled = jnp.sum(select, axis=2)
    got_codes = pick_pages(every, which, filled.reshape(owners * capacity), capacity)
    got_steps = jnp.sum(
        select.astype(jnp.float32) * every_steps.astype(jnp.float32)[:, None, :], axis=2
    ).astype(jnp.bfloat16)
    return (
        rotated,
        got_codes.reshape(1, owners, capacity, 1, PAGE, head_dim),
        got_steps.reshape(1, owners, capacity, 1),
    )


def solution(mesh):
    in_specs = (
        P("req", None, "tp"),
        P("req", None, "tp", None),
        P("tp"),
        P("req", None, None),
        P("req"),
    )
    out_specs = (
        P("req", None, "tp"),
        P("req", None, None, "tp", None, None),
        P("req", None, None, "tp"),
    )
    return jax.shard_map(body, mesh=mesh, in_specs=in_specs, out_specs=out_specs, check_vma=False)
```

```python
import functools
import math

import jax
import jax.numpy as jnp
from jax import lax
from jax.experimental import pallas as pl
from jax.experimental.pallas import tpu as pltpu
from jax.sharding import PartitionSpec as P

PAGE = 16
BLOCK = 128


def attend_kernel(length_ref, q_ref, kv_ref, out_ref, k_ref, v_ref, *, blocks, heads):
    head_dim = k_ref.shape[1]
    seq_len = k_ref.shape[0]
    step = pl.program_id(0)

    @pl.when(step == 0)
    def _():
        k_ref[...] = kv_ref[:, 0].reshape(seq_len, head_dim)
        v_ref[:, :head_dim] = kv_ref[:, 1].reshape(seq_len, head_dim)
        v_ref[:, head_dim:] = jnp.ones((seq_len, head_dim), jnp.bfloat16)

    rate = math.log2(math.e) / math.sqrt(head_dim)
    rows = lax.broadcasted_iota(jnp.int32, (BLOCK, BLOCK), 0)
    cols = lax.broadcasted_iota(jnp.int32, (BLOCK, BLOCK), 1)
    causal = rows >= cols
    live = step * BLOCK + lax.broadcasted_iota(jnp.int32, (BLOCK, head_dim), 0) < length_ref[0]

    def attend(index):
        finish = (index + 1) * BLOCK
        for head in range(heads):
            columns = slice(head * head_dim, (head + 1) * head_dim)
            scores = lax.dot_general(
                q_ref[:, columns],
                k_ref[:finish],
                (((1,), (1,)), ((), ())),
                preferred_element_type=jnp.float32,
            )
            last = jnp.where(causal, scores[:, index * BLOCK :], -jnp.inf)
            if index:
                scores = jnp.concatenate([scores[:, : index * BLOCK], last], axis=1)
            else:
                scores = last
            top = jnp.max(scores, axis=1, keepdims=True)
            weights = jnp.exp2((scores - top) * rate).astype(jnp.bfloat16)
            both = jnp.dot(weights, v_ref[:finish], preferred_element_type=jnp.float32)
            attended = both[:, :head_dim] / both[:, head_dim:]
            out_ref[:, columns] = jnp.where(live, attended, 0.0).astype(jnp.bfloat16)

    for index in range(blocks):
        pl.when(step == index)(functools.partial(attend, index))


def attend_local(queries, received, length, head_dim):
    seq_len, width = queries.shape
    heads = width // head_dim
    blocks = seq_len // BLOCK
    return pl.pallas_call(
        functools.partial(attend_kernel, blocks=blocks, heads=heads),
        grid=(blocks,),
        in_specs=[
            pl.BlockSpec(memory_space=pltpu.SMEM),
            pl.BlockSpec((BLOCK, width), lambda i: (i, 0)),
            pl.BlockSpec(received.shape, lambda i: (0, 0, 0, 0)),
        ],
        out_specs=pl.BlockSpec((BLOCK, width), lambda i: (i, 0)),
        out_shape=jax.ShapeDtypeStruct((seq_len, width), jnp.bfloat16),
        scratch_shapes=[
            pltpu.VMEM((seq_len, head_dim), jnp.bfloat16),
            pltpu.VMEM((seq_len, 2 * head_dim), jnp.bfloat16),
        ],
        compiler_params=pltpu.CompilerParams(vmem_limit_bytes=32 * 1024 * 1024),
        cost_estimate=pl.CostEstimate(
            flops=4 * seq_len * seq_len * width,
            bytes_accessed=4 * seq_len * width,
            transcendentals=seq_len * seq_len * heads,
        ),
        name="attend",
    )(length, queries, received)


def butterflies(values):
    values = list(values)
    stride = 1
    while stride < len(values):
        for low in range(len(values)):
            if not low & stride:
                a, b = values[low], values[low + stride]
                values[low], values[low + stride] = a + b, a - b
        stride *= 2
    return values


def hadamard_kernel(in_ref, out_ref, mid_ref, *, heads):
    devices, tokens, width = in_ref.shape
    head_dim = width // heads
    factor = 1.0 / math.sqrt(devices * heads)
    columns = [slice(h * head_dim, (h + 1) * head_dim) for h in range(heads)]
    for first in range(0, tokens, PAGE):
        rows = slice(first, first + PAGE)
        for device in range(devices):
            tiles = butterflies([in_ref[device, rows, c].astype(jnp.float32) for c in columns])
            for c, tile in zip(columns, tiles):
                mid_ref[device, :, c] = tile
        for c in columns:
            tiles = butterflies([mid_ref[device, :, c] for device in range(devices)])
            for device, tile in enumerate(tiles):
                out_ref[device, rows, c] = (tile * factor).astype(jnp.bfloat16)


def hadamard(blocks, heads):
    devices, tokens, width = blocks.shape
    spec = pl.BlockSpec((devices, PAGE, width), lambda i: (0, i, 0))
    return pl.pallas_call(
        functools.partial(hadamard_kernel, heads=heads),
        grid=(tokens // PAGE,),
        in_specs=[spec],
        out_specs=spec,
        out_shape=jax.ShapeDtypeStruct(blocks.shape, jnp.bfloat16),
        scratch_shapes=[pltpu.VMEM((devices, PAGE, width), jnp.float32)],
        compiler_params=pltpu.CompilerParams(vmem_limit_bytes=32 * 1024 * 1024),
        cost_estimate=pl.CostEstimate(
            flops=7 * blocks.size, bytes_accessed=4 * blocks.size, transcendentals=0
        ),
        name="hadamard",
    )(blocks)


def page_kernel(
    length_ref, level_ref, side_ref, owner_ref, kv_ref, out_ref, count_ref, *, owners, capacity
):
    sources, _, tokens, head_dim = kv_ref.shape
    out_ref[...] = jnp.zeros_like(out_ref)
    for owner in range(owners):
        count_ref[owner] = 0
    level = level_ref[0].astype(jnp.float32)
    side = side_ref[0]
    rows = lax.broadcasted_iota(jnp.int32, (PAGE, head_dim), 0)
    tail = lax.broadcasted_iota(jnp.int32, (8, head_dim), 0)
    per_source = tokens // PAGE

    def one_page(page, _):
        source = page // per_source
        first = (page % per_source) * PAGE
        values = kv_ref[source, side, pl.ds(pl.multiple_of(first, PAGE), PAGE), :]
        live = page * PAGE + rows < length_ref[0]
        values = jnp.where(live, values.astype(jnp.float32), 0.0)
        total = jnp.sum(values * values, axis=(0, 1), keepdims=True)
        rms = jnp.sqrt(total / (PAGE * head_dim) + 1e-06)
        step = (rms * 0.5).astype(jnp.bfloat16).astype(jnp.float32)
        codes = jnp.clip(values / step, -level, level).astype(jnp.bfloat16)
        owner = owner_ref[page]
        slot = jnp.minimum(count_ref[owner], capacity - 1)
        count_ref[owner] = slot + 1
        out_ref[owner, pl.ds(pl.multiple_of(slot * PAGE, PAGE), PAGE), :] = codes
        before = out_ref[owner, capacity * PAGE :, :].astype(jnp.float32)
        steps = jnp.where(tail == slot, jnp.broadcast_to(step, tail.shape), before)
        out_ref[owner, capacity * PAGE :, :] = steps.astype(jnp.bfloat16)
        return 0

    lax.fori_loop(0, sources * per_source, one_page, 0)


def page_table(received, length, level, owner_of, owners, capacity):
    head_dim = received.shape[3]
    smem = pl.BlockSpec(memory_space=pltpu.SMEM)
    vmem = pl.BlockSpec(memory_space=pltpu.VMEM)
    side = (lax.axis_index("tp") % 2).astype(jnp.int32).reshape(1)
    shape = (owners, capacity * PAGE + 8, head_dim)
    return pl.pallas_call(
        functools.partial(page_kernel, owners=owners, capacity=capacity),
        in_specs=[smem, smem, smem, smem, vmem],
        out_specs=vmem,
        out_shape=jax.ShapeDtypeStruct(shape, jnp.bfloat16),
        scratch_shapes=[pltpu.SMEM((owners,), jnp.int32)],
        compiler_params=pltpu.CompilerParams(vmem_limit_bytes=32 * 1024 * 1024),
        cost_estimate=pl.CostEstimate(
            flops=10 * received.size, bytes_accessed=2 * received.size, transcendentals=0
        ),
        name="pages",
    )(length, level, side, owner_of, received)


def to_owners(table, axis):
    count = lax.axis_size(axis)
    position = lax.axis_index(axis)
    inner = table.shape[1:]
    for bit in range(count.bit_length() - 1):
        stride = 1 << bit
        upper = jnp.right_shift(position, bit) % 2
        halves = table.reshape((count // (2 * stride), 2, stride) + inner)
        keep = lax.dynamic_index_in_dim(halves, upper, 1, keepdims=False)
        send = lax.dynamic_index_in_dim(halves, 1 - upper, 1, keepdims=False)
        got = lax.ppermute(send, axis, [(i, i ^ stride) for i in range(count)])
        low = jnp.where(upper == 0, keep, got)
        high = jnp.where(upper == 0, got, keep)
        table = jnp.stack([low, high], axis=1).reshape((count,) + inner)
    return table


def body(queries, kv_heads, bit_widths, destinations, lengths):
    local_kv = kv_heads[0]
    total_rows, tok_here, head_dim = local_kv.shape
    tp_count = lax.axis_size("tp")
    owners = lax.axis_size("req")
    paired = local_kv.reshape(total_rows // 2, 2, tok_here, head_dim)
    outgoing = jnp.repeat(paired, tp_count // (total_rows // 2), axis=0)
    received = lax.all_to_all(outgoing, "tp", split_axis=0, concat_axis=0, tiled=True)
    seq_len = tp_count * tok_here
    heads_here = queries.shape[2] // head_dim

    attended = attend_local(queries[0], received, lengths, head_dim)
    blocks = attended.reshape(tp_count, seq_len // tp_count, heads_here * head_dim)
    blocks = lax.all_to_all(blocks, "tp", split_axis=0, concat_axis=0, tiled=True)
    mixed = hadamard(blocks, heads_here)
    back = lax.all_to_all(mixed, "tp", split_axis=0, concat_axis=0, tiled=True)
    rotated = back.reshape(1, seq_len, heads_here * head_dim)

    pages = seq_len // PAGE
    capacity = max(2, (3 * pages + 2 * owners - 1) // (2 * owners))
    level = 2 ** (bit_widths - 1) - 1
    table = page_table(received, lengths, level, destinations[0, :, 0], owners, capacity)
    table = to_owners(table, "req")
    got_codes = table[:, : capacity * PAGE].reshape(1, owners, capacity, 1, PAGE, head_dim)
    got_steps = table[:, capacity * PAGE : capacity * (PAGE + 1), 0]
    return rotated, got_codes, got_steps.reshape(1, owners, capacity, 1)


def solution(mesh):
    in_specs = (
        P("req", None, "tp"),
        P("req", None, "tp", None),
        P("tp"),
        P("req", None, None),
        P("req"),
    )
    out_specs = (
        P("req", None, "tp"),
        P("req", None, None, "tp", None, None),
        P("req", None, None, "tp"),
    )
    return jax.shard_map(body, mesh=mesh, in_specs=in_specs, out_specs=out_specs, check_vma=False)
```

```python
import functools
import math

import jax
import jax.numpy as jnp
from jax import lax
from jax.experimental import pallas as pl
from jax.experimental.pallas import tpu as pltpu
from jax.sharding import PartitionSpec as P

PAGE = 16
EARLY = 3
BLOCK = 128


def attend_kernel(length_ref, q_ref, kv_ref, after_ref, out_ref, k_ref, v_ref, *, blocks, heads):
    del after_ref
    head_dim = k_ref.shape[1]
    seq_len = k_ref.shape[0]
    step = pl.program_id(0)

    @pl.when(step == 0)
    def _():
        k_ref[...] = kv_ref[:, 0].reshape(seq_len, head_dim)
        v_ref[:, :head_dim] = kv_ref[:, 1].reshape(seq_len, head_dim)
        v_ref[:, head_dim:] = jnp.ones((seq_len, head_dim), jnp.bfloat16)

    rate = math.log2(math.e) / math.sqrt(head_dim)
    rows = lax.broadcasted_iota(jnp.int32, (BLOCK, BLOCK), 0)
    cols = lax.broadcasted_iota(jnp.int32, (BLOCK, BLOCK), 1)
    causal = rows >= cols
    live = step * BLOCK + lax.broadcasted_iota(jnp.int32, (BLOCK, head_dim), 0) < length_ref[0]

    def attend(index):
        finish = (index + 1) * BLOCK
        for head in range(heads):
            columns = slice(head * head_dim, (head + 1) * head_dim)
            scores = lax.dot_general(
                q_ref[:, columns],
                k_ref[:finish],
                (((1,), (1,)), ((), ())),
                preferred_element_type=jnp.float32,
            )
            last = jnp.where(causal, scores[:, index * BLOCK :], -jnp.inf)
            if index:
                scores = jnp.concatenate([scores[:, : index * BLOCK], last], axis=1)
            else:
                scores = last
            top = jnp.max(scores, axis=1, keepdims=True)
            weights = jnp.exp2((scores - top) * rate).astype(jnp.bfloat16)
            both = jnp.dot(weights, v_ref[:finish], preferred_element_type=jnp.float32)
            attended = both[:, :head_dim] / both[:, head_dim:]
            out_ref[:, columns] = jnp.where(live, attended, 0.0).astype(jnp.bfloat16)

    for index in range(blocks):
        pl.when(step == index)(functools.partial(attend, index))


def attend_local(queries, received, length, head_dim, after):
    seq_len, width = queries.shape
    heads = width // head_dim
    blocks = seq_len // BLOCK
    return pl.pallas_call(
        functools.partial(attend_kernel, blocks=blocks, heads=heads),
        grid=(blocks,),
        in_specs=[
            pl.BlockSpec(memory_space=pltpu.SMEM),
            pl.BlockSpec((BLOCK, width), lambda i: (i, 0)),
            pl.BlockSpec(received.shape, lambda i: (0, 0, 0, 0)),
            pl.BlockSpec(memory_space=pl.ANY),
        ],
        out_specs=pl.BlockSpec((BLOCK, width), lambda i: (i, 0)),
        out_shape=jax.ShapeDtypeStruct((seq_len, width), jnp.bfloat16),
        scratch_shapes=[
            pltpu.VMEM((seq_len, head_dim), jnp.bfloat16),
            pltpu.VMEM((seq_len, 2 * head_dim), jnp.bfloat16),
        ],
        compiler_params=pltpu.CompilerParams(vmem_limit_bytes=32 * 1024 * 1024),
        cost_estimate=pl.CostEstimate(
            flops=4 * seq_len * seq_len * width,
            bytes_accessed=4 * seq_len * width,
            transcendentals=seq_len * seq_len * heads,
        ),
        name="attend",
    )(length, queries, received, after)


def butterflies(values):
    values = list(values)
    stride = 1
    while stride < len(values):
        for low in range(len(values)):
            if not low & stride:
                a, b = values[low], values[low + stride]
                values[low], values[low + stride] = a + b, a - b
        stride *= 2
    return values


def hadamard_kernel(in_ref, after_ref, out_ref, mid_ref, *, heads):
    del after_ref
    devices, tokens, width = in_ref.shape
    head_dim = width // heads
    factor = 1.0 / math.sqrt(devices * heads)
    columns = [slice(h * head_dim, (h + 1) * head_dim) for h in range(heads)]
    for first in range(0, tokens, PAGE):
        rows = slice(first, first + PAGE)
        for device in range(devices):
            tiles = butterflies([in_ref[device, rows, c].astype(jnp.float32) for c in columns])
            for c, tile in zip(columns, tiles):
                mid_ref[device, :, c] = tile
        for c in columns:
            tiles = butterflies([mid_ref[device, :, c] for device in range(devices)])
            for device, tile in enumerate(tiles):
                out_ref[device, rows, c] = (tile * factor).astype(jnp.bfloat16)


def hadamard(blocks, heads, after):
    devices, tokens, width = blocks.shape
    spec = pl.BlockSpec((devices, PAGE, width), lambda i: (0, i, 0))
    return pl.pallas_call(
        functools.partial(hadamard_kernel, heads=heads),
        grid=(tokens // PAGE,),
        in_specs=[spec, pl.BlockSpec(memory_space=pl.ANY)],
        out_specs=spec,
        out_shape=jax.ShapeDtypeStruct(blocks.shape, jnp.bfloat16),
        scratch_shapes=[pltpu.VMEM((devices, PAGE, width), jnp.float32)],
        compiler_params=pltpu.CompilerParams(vmem_limit_bytes=32 * 1024 * 1024),
        cost_estimate=pl.CostEstimate(
            flops=7 * blocks.size, bytes_accessed=4 * blocks.size, transcendentals=0
        ),
        name="hadamard",
    )(blocks, after)


def page_kernel(
    length_ref, level_ref, side_ref, owner_ref, kv_ref, out_ref, count_ref, slot_ref, *, capacity
):
    sources, _, tokens, head_dim = kv_ref.shape
    owners = out_ref.shape[0]
    per_source = tokens // PAGE
    out_ref[...] = jnp.zeros_like(out_ref)
    level = level_ref[0].astype(jnp.float32)
    side = side_ref[0]
    rows = lax.broadcasted_iota(jnp.int32, (PAGE, head_dim), 0)
    tail = lax.broadcasted_iota(jnp.int32, (8, head_dim), 0)
    for owner in range(owners):
        count_ref[owner] = 0
    for page in range(sources * per_source):
        owner = owner_ref[page]
        slot_ref[page] = jnp.minimum(count_ref[owner], capacity - 1)
        count_ref[owner] = count_ref[owner] + 1

    for page in range(sources * per_source):
        part = page % per_source
        values = kv_ref[page // per_source, side, part * PAGE : (part + 1) * PAGE, :]
        values = jnp.where(page * PAGE + rows < length_ref[0], values.astype(jnp.float32), 0.0)
        total = jnp.sum(values * values, axis=(0, 1), keepdims=True)
        rms = jnp.sqrt(total / (PAGE * head_dim) + 1e-06)
        step = (rms * 0.5).astype(jnp.bfloat16).astype(jnp.float32)
        codes = jnp.clip(values / step, -level, level).astype(jnp.bfloat16)
        owner = owner_ref[page]
        slot = slot_ref[page]
        out_ref[owner, pl.ds(pl.multiple_of(slot * PAGE, PAGE), PAGE), :] = codes
        before = out_ref[owner, capacity * PAGE :, :].astype(jnp.float32)
        steps = jnp.where(tail == slot, jnp.broadcast_to(step, tail.shape), before)
        out_ref[owner, capacity * PAGE :, :] = steps.astype(jnp.bfloat16)


def page_table(received, length, level, owner_of, owners, capacity):
    head_dim = received.shape[3]
    smem = pl.BlockSpec(memory_space=pltpu.SMEM)
    vmem = pl.BlockSpec(memory_space=pltpu.VMEM)
    side = (lax.axis_index("tp") % 2).astype(jnp.int32).reshape(1)
    shape = (owners, capacity * PAGE + 8, head_dim)
    return pl.pallas_call(
        functools.partial(page_kernel, capacity=capacity),
        in_specs=[smem, smem, smem, smem, vmem],
        out_specs=vmem,
        out_shape=jax.ShapeDtypeStruct(shape, jnp.bfloat16),
        scratch_shapes=[
            pltpu.SMEM((owners,), jnp.int32),
            pltpu.SMEM(owner_of.shape, jnp.int32),
        ],
        compiler_params=pltpu.CompilerParams(vmem_limit_bytes=32 * 1024 * 1024),
        cost_estimate=pl.CostEstimate(
            flops=10 * received.size, bytes_accessed=2 * received.size, transcendentals=0
        ),
        name="pages",
    )(length, level, side, owner_of, received)


def to_owners(table, axis, bits, members):
    count = lax.axis_size(axis)
    position = lax.axis_index(axis)
    inner = table.shape[1:]
    for bit in bits:
        stride = 1 << bit
        upper = jnp.right_shift(position, bit) % 2
        halves = table.reshape((count // (2 * stride), 2, stride) + inner)
        keep = lax.dynamic_index_in_dim(halves, upper, 1, keepdims=False)
        send = lax.dynamic_index_in_dim(halves, 1 - upper, 1, keepdims=False)
        got = lax.ppermute(send, axis, [(i, i ^ stride) for i in members])
        low = jnp.where(upper == 0, keep, got)
        high = jnp.where(upper == 0, got, keep)
        table = jnp.stack([low, high], axis=1).reshape((count,) + inner)
    return table


def body(queries, kv_heads, bit_widths, destinations, lengths):
    local_kv = kv_heads[0]
    total_rows, tok_here, head_dim = local_kv.shape
    tp_count = lax.axis_size("tp")
    owners = lax.axis_size("req")
    paired = local_kv.reshape(total_rows // 2, 2, tok_here, head_dim)
    outgoing = jnp.repeat(paired, tp_count // (total_rows // 2), axis=0)
    received = lax.all_to_all(outgoing, "tp", split_axis=0, concat_axis=0, tiled=True)
    seq_len = tp_count * tok_here
    heads_here = queries.shape[2] // head_dim

    pages = seq_len // PAGE
    capacity = max(2, (3 * pages + 2 * owners - 1) // (2 * owners))
    level = 2 ** (bit_widths - 1) - 1
    bits = list(range(1, owners.bit_length() - 1)) + [0]
    first_bits, last_bits = bits[:EARLY], bits[EARLY:]
    odd = lax.axis_index("req") % 2 == 1

    def start_pages(members):
        table = page_table(received, lengths, level, destinations[0, :, 0], owners, capacity)
        return to_owners(table, "req", first_bits, members)

    shape = (owners, capacity * PAGE + 8, head_dim)
    table = lax.cond(
        odd,
        lambda: start_pages(range(1, owners, 2)),
        lambda: jnp.zeros(shape, jnp.bfloat16),
    )
    attended = attend_local(queries[0], received, lengths, head_dim, table)
    blocks = attended.reshape(tp_count, seq_len // tp_count, heads_here * head_dim)
    blocks = lax.all_to_all(blocks, "tp", split_axis=0, concat_axis=0, tiled=True)
    table = lax.cond(odd, lambda t: t, lambda t: start_pages(range(0, owners, 2)), table)
    mixed = hadamard(blocks, heads_here, table)
    back = lax.all_to_all(mixed, "tp", split_axis=0, concat_axis=0, tiled=True)
    rotated = back.reshape(1, seq_len, heads_here * head_dim)
    table = to_owners(table, "req", last_bits, range(owners))
    got_codes = table[:, : capacity * PAGE].reshape(1, owners, capacity, 1, PAGE, head_dim)
    got_steps = table[:, capacity * PAGE : capacity * (PAGE + 1), 0]
    return rotated, got_codes, got_steps.reshape(1, owners, capacity, 1)


def solution(mesh):
    in_specs = (
        P("req", None, "tp"),
        P("req", None, "tp", None),
        P("tp"),
        P("req", None, None),
        P("req"),
    )
    out_specs = (
        P("req", None, "tp"),
        P("req", None, None, "tp", None, None),
        P("req", None, None, "tp"),
    )
    return jax.shard_map(body, mesh=mesh, in_specs=in_specs, out_specs=out_specs, check_vma=False)
```

```python
import functools
import math

import jax
import jax.numpy as jnp
from jax import lax
from jax.experimental import pallas as pl
from jax.experimental.pallas import tpu as pltpu
from jax.sharding import PartitionSpec as P

PAGE = 16
EARLY = 3
SMEM = pl.BlockSpec(memory_space=pltpu.SMEM)
VMEM = pl.BlockSpec(memory_space=pltpu.VMEM)
ANYWHERE = pl.BlockSpec(memory_space=pl.ANY)
BLOCK = 256


def attend_kernel(
    length_ref, q_hbm, kv_ref, after_ref, out_hbm, q_ref, out_ref, sems, k_ref, v_ref, *, heads
):
    del after_ref
    seq_len, head_dim = k_ref.shape
    parts = [slice(first, first + BLOCK) for first in range(0, seq_len, BLOCK)]
    fetches = [
        pltpu.make_async_copy(q_hbm.at[part], q_ref.at[part], sems.at[0, index])
        for index, part in enumerate(parts)
    ]
    writes = [
        pltpu.make_async_copy(out_ref.at[part], out_hbm.at[part], sems.at[1, index])
        for index, part in enumerate(parts)
    ]
    for fetch in fetches:
        fetch.start()
    k_ref[...] = kv_ref[:, 0].reshape(seq_len, head_dim)
    v_ref[:, :head_dim] = kv_ref[:, 1].reshape(seq_len, head_dim)
    v_ref[:, head_dim:] = jnp.ones((seq_len, head_dim), jnp.bfloat16)
    rate = math.log2(math.e) / math.sqrt(head_dim)
    rows = lax.broadcasted_iota(jnp.int32, (BLOCK, BLOCK), 0)
    cols = lax.broadcasted_iota(jnp.int32, (BLOCK, BLOCK), 1)
    causal = rows >= cols
    row = lax.broadcasted_iota(jnp.int32, (BLOCK, head_dim), 0)

    for index, part in enumerate(parts):
        fetches[index].wait()
        start, finish = part.start, part.stop
        live = row + start < length_ref[0]
        for column in range(0, heads * head_dim, head_dim):
            columns = slice(column, column + head_dim)
            scores = lax.dot_general(
                q_ref[part, columns],
                k_ref[:finish],
                (((1,), (1,)), ((), ())),
                preferred_element_type=jnp.float32,
            )
            last = jnp.where(causal, scores[:, start:], -jnp.inf)
            scores = jnp.concatenate([scores[:, :start], last], axis=1) if start else last
            top = jnp.max(scores, axis=1, keepdims=True)
            weights = jnp.exp2((scores - top) * rate).astype(jnp.bfloat16)
            both = jnp.dot(weights, v_ref[:finish], preferred_element_type=jnp.float32)
            attended = both[:, :head_dim] / both[:, head_dim:]
            out_ref[part, columns] = jnp.where(live, attended, 0.0).astype(jnp.bfloat16)
        writes[index].start()
    for write in writes:
        write.wait()


def attend_local(queries, received, length, head_dim, after):
    seq_len, width = queries.shape
    heads = width // head_dim
    return pl.pallas_call(
        functools.partial(attend_kernel, heads=heads),
        in_specs=[SMEM, ANYWHERE, VMEM, ANYWHERE],
        out_specs=ANYWHERE,
        out_shape=jax.ShapeDtypeStruct((seq_len, width), jnp.bfloat16),
        scratch_shapes=[
            pltpu.VMEM((seq_len, width), jnp.bfloat16),
            pltpu.VMEM((seq_len, width), jnp.bfloat16),
            pltpu.SemaphoreType.DMA((2, seq_len // BLOCK)),
            pltpu.VMEM((seq_len, head_dim), jnp.bfloat16),
            pltpu.VMEM((seq_len, 2 * head_dim), jnp.bfloat16),
        ],
        compiler_params=pltpu.CompilerParams(vmem_limit_bytes=62 * 1024 * 1024),
        cost_estimate=pl.CostEstimate(
            flops=4 * seq_len * seq_len * width,
            bytes_accessed=4 * seq_len * width,
            transcendentals=seq_len * seq_len * heads,
        ),
        name="attend",
    )(length, queries, received, after)


def placeholder(shape):
    def nothing(out_ref):
        del out_ref

    return pl.pallas_call(
        nothing,
        out_specs=pl.BlockSpec(memory_space=pl.ANY),
        out_shape=jax.ShapeDtypeStruct(shape, jnp.bfloat16),
        name="placeholder",
    )()


def butterflies(values):
    values = list(values)
    stride = 1
    while stride < len(values):
        for low in range(len(values)):
            if not low & stride:
                a, b = values[low], values[low + stride]
                values[low], values[low + stride] = a + b, a - b
        stride *= 2
    return values


def hadamard_kernel(in_ref, after_ref, out_ref, mid_ref, *, heads):
    del after_ref
    devices, tokens, width = in_ref.shape
    head_dim = width // heads
    factor = 1.0 / math.sqrt(devices * heads)
    columns = [slice(h * head_dim, (h + 1) * head_dim) for h in range(heads)]
    for first in range(0, tokens, PAGE):
        rows = slice(first, first + PAGE)
        for device in range(devices):
            tiles = butterflies([in_ref[device, rows, c].astype(jnp.float32) for c in columns])
            for c, tile in zip(columns, tiles):
                mid_ref[device, :, c] = tile
        for c in columns:
            tiles = butterflies([mid_ref[device, :, c] for device in range(devices)])
            for device, tile in enumerate(tiles):
                out_ref[device, rows, c] = (tile * factor).astype(jnp.bfloat16)


def hadamard(blocks, heads, after):
    devices, tokens, width = blocks.shape
    spec = pl.BlockSpec((devices, PAGE, width), lambda i: (0, i, 0))
    return pl.pallas_call(
        functools.partial(hadamard_kernel, heads=heads),
        grid=(tokens // PAGE,),
        in_specs=[spec, pl.BlockSpec(memory_space=pl.ANY)],
        out_specs=spec,
        out_shape=jax.ShapeDtypeStruct(blocks.shape, jnp.bfloat16),
        scratch_shapes=[pltpu.VMEM((devices, PAGE, width), jnp.float32)],
        compiler_params=pltpu.CompilerParams(vmem_limit_bytes=32 * 1024 * 1024),
        cost_estimate=pl.CostEstimate(
            flops=7 * blocks.size, bytes_accessed=4 * blocks.size, transcendentals=0
        ),
        name="hadamard",
    )(blocks, after)


def page_kernel(
    length_ref, level_ref, side_ref, owner_ref, kv_ref, out_ref, count_ref, slot_ref, *, capacity
):
    sources, _, tokens, head_dim = kv_ref.shape
    owners = out_ref.shape[0]
    per_source = tokens // PAGE
    out_ref[...] = jnp.zeros_like(out_ref)
    level = level_ref[0].astype(jnp.float32)
    side = side_ref[0]
    rows = lax.broadcasted_iota(jnp.int32, (PAGE, head_dim), 0)
    tail = lax.broadcasted_iota(jnp.int32, (8, head_dim), 0)
    for owner in range(owners):
        count_ref[owner] = 0
    for page in range(sources * per_source):
        owner = owner_ref[page]
        slot_ref[page] = jnp.minimum(count_ref[owner], capacity - 1)
        count_ref[owner] = count_ref[owner] + 1

    for page in range(sources * per_source):
        part = page % per_source
        values = kv_ref[page // per_source, side, part * PAGE : (part + 1) * PAGE, :]
        values = jnp.where(page * PAGE + rows < length_ref[0], values.astype(jnp.float32), 0.0)
        total = jnp.sum(values * values, axis=(0, 1), keepdims=True)
        rms = jnp.sqrt(total / (PAGE * head_dim) + 1e-06)
        step = (rms * 0.5).astype(jnp.bfloat16).astype(jnp.float32)
        codes = jnp.clip(values / step, -level, level).astype(jnp.bfloat16)
        owner = owner_ref[page]
        slot = slot_ref[page]
        out_ref[owner, pl.ds(pl.multiple_of(slot * PAGE, PAGE), PAGE), :] = codes
        before = out_ref[owner, capacity * PAGE :, :].astype(jnp.float32)
        steps = jnp.where(tail == slot, jnp.broadcast_to(step, tail.shape), before)
        out_ref[owner, capacity * PAGE :, :] = steps.astype(jnp.bfloat16)


def page_table(received, length, level, owner_of, owners, capacity):
    head_dim = received.shape[3]
    smem = pl.BlockSpec(memory_space=pltpu.SMEM)
    vmem = pl.BlockSpec(memory_space=pltpu.VMEM)
    side = (lax.axis_index("tp") % 2).astype(jnp.int32).reshape(1)
    shape = (owners, capacity * PAGE + 8, head_dim)
    return pl.pallas_call(
        functools.partial(page_kernel, capacity=capacity),
        in_specs=[smem, smem, smem, smem, vmem],
        out_specs=vmem,
        out_shape=jax.ShapeDtypeStruct(shape, jnp.bfloat16),
        scratch_shapes=[
            pltpu.SMEM((owners,), jnp.int32),
            pltpu.SMEM(owner_of.shape, jnp.int32),
        ],
        compiler_params=pltpu.CompilerParams(vmem_limit_bytes=32 * 1024 * 1024),
        cost_estimate=pl.CostEstimate(
            flops=10 * received.size, bytes_accessed=2 * received.size, transcendentals=0
        ),
        name="pages",
    )(length, level, side, owner_of, received)


def to_owners(table, axis, bits, members):
    count = lax.axis_size(axis)
    position = lax.axis_index(axis)
    inner = table.shape[1:]
    for bit in bits:
        stride = 1 << bit
        upper = jnp.right_shift(position, bit) % 2
        halves = table.reshape((count // (2 * stride), 2, stride) + inner)
        keep = lax.dynamic_index_in_dim(halves, upper, 1, keepdims=False)
        send = lax.dynamic_index_in_dim(halves, 1 - upper, 1, keepdims=False)
        got = lax.ppermute(send, axis, [(i, i ^ stride) for i in members])
        low = jnp.where(upper == 0, keep, got)
        high = jnp.where(upper == 0, got, keep)
        table = jnp.stack([low, high], axis=1).reshape((count,) + inner)
    return table


def body(queries, kv_heads, bit_widths, destinations, lengths):
    local_kv = kv_heads[0]
    total_rows, tok_here, head_dim = local_kv.shape
    tp_count = lax.axis_size("tp")
    owners = lax.axis_size("req")
    paired = local_kv.reshape(total_rows // 2, 2, tok_here, head_dim)
    outgoing = jnp.repeat(paired, tp_count // (total_rows // 2), axis=0)
    received = lax.all_to_all(outgoing, "tp", split_axis=0, concat_axis=0, tiled=True)
    seq_len = tp_count * tok_here
    heads_here = queries.shape[2] // head_dim

    pages = seq_len // PAGE
    capacity = max(2, (3 * pages + 2 * owners - 1) // (2 * owners))
    level = 2 ** (bit_widths - 1) - 1
    bits = list(range(1, owners.bit_length() - 1)) + [0]
    first_bits, last_bits = bits[:EARLY], bits[EARLY:]
    odd = lax.axis_index("req") % 2 == 1

    def start_pages(members):
        table = page_table(received, lengths, level, destinations[0, :, 0], owners, capacity)
        return to_owners(table, "req", first_bits, members)

    shape = (owners, capacity * PAGE + 8, head_dim)
    table = lax.cond(
        odd,
        lambda: start_pages(range(1, owners, 2)),
        lambda: placeholder(shape),
    )
    attended = attend_local(queries[0], received, lengths, head_dim, table)
    blocks = attended.reshape(tp_count, seq_len // tp_count, heads_here * head_dim)
    blocks = lax.all_to_all(blocks, "tp", split_axis=0, concat_axis=0, tiled=True)
    table = lax.cond(odd, lambda t: t, lambda t: start_pages(range(0, owners, 2)), table)
    mixed = hadamard(blocks, heads_here, table)
    back = lax.all_to_all(mixed, "tp", split_axis=0, concat_axis=0, tiled=True)
    rotated = back.reshape(1, seq_len, heads_here * head_dim)
    table = to_owners(table, "req", last_bits, range(owners))
    got_codes = table[:, : capacity * PAGE].reshape(1, owners, capacity, 1, PAGE, head_dim)
    got_steps = table[:, capacity * PAGE : capacity * (PAGE + 1), 0]
    return rotated, got_codes, got_steps.reshape(1, owners, capacity, 1)


def solution(mesh):
    in_specs = (
        P("req", None, "tp"),
        P("req", None, "tp", None),
        P("tp"),
        P("req", None, None),
        P("req"),
    )
    out_specs = (
        P("req", None, "tp"),
        P("req", None, None, "tp", None, None),
        P("req", None, None, "tp"),
    )
    return jax.shard_map(body, mesh=mesh, in_specs=in_specs, out_specs=out_specs, check_vma=False)
```

```python
import functools
import math

import jax
import jax.numpy as jnp
from jax import lax
from jax.experimental import pallas as pl
from jax.experimental.pallas import tpu as pltpu
from jax.sharding import PartitionSpec as P

PAGE = 16
EARLY = 3
SMEM = pl.BlockSpec(memory_space=pltpu.SMEM)
VMEM = pl.BlockSpec(memory_space=pltpu.VMEM)
ANYWHERE = pl.BlockSpec(memory_space=pl.ANY)
BLOCK = 256


def attend_kernel(
    length_ref, q_hbm, kv_ref, after_ref, out_hbm, q_ref, out_ref, sems, k_ref, v_ref, *, heads
):
    del after_ref
    seq_len, head_dim = k_ref.shape
    parts = [slice(first, first + BLOCK) for first in range(0, seq_len, BLOCK)]
    fetches = [
        pltpu.make_async_copy(q_hbm.at[part], q_ref.at[part], sems.at[0, index])
        for index, part in enumerate(parts)
    ]
    writes = [
        pltpu.make_async_copy(out_ref.at[part], out_hbm.at[part], sems.at[1, index])
        for index, part in enumerate(parts)
    ]
    for fetch in fetches:
        fetch.start()
    k_ref[...] = kv_ref[:, 0].reshape(seq_len, head_dim)
    v_ref[:, :head_dim] = kv_ref[:, 1].reshape(seq_len, head_dim)
    v_ref[:, head_dim:] = jnp.ones((seq_len, head_dim), jnp.bfloat16)
    rate = math.log2(math.e) / math.sqrt(head_dim)
    rows = lax.broadcasted_iota(jnp.int32, (BLOCK, BLOCK), 0)
    cols = lax.broadcasted_iota(jnp.int32, (BLOCK, BLOCK), 1)
    causal = rows >= cols
    row = lax.broadcasted_iota(jnp.int32, (BLOCK, head_dim), 0)

    for index, part in enumerate(parts):
        fetches[index].wait()
        start, finish = part.start, part.stop
        live = row + start < length_ref[0]
        for column in range(0, heads * head_dim, head_dim):
            columns = slice(column, column + head_dim)
            scores = lax.dot_general(
                q_ref[part, columns],
                k_ref[:finish],
                (((1,), (1,)), ((), ())),
                preferred_element_type=jnp.float32,
            )
            last = jnp.where(causal, scores[:, start:], -jnp.inf)
            scores = jnp.concatenate([scores[:, :start], last], axis=1) if start else last
            top = jnp.max(scores, axis=1, keepdims=True)
            weights = jnp.exp2((scores - top) * rate).astype(jnp.bfloat16)
            both = jnp.dot(weights, v_ref[:finish], preferred_element_type=jnp.float32)
            attended = both[:, :head_dim] / both[:, head_dim:]
            out_ref[part, columns] = jnp.where(live, attended, 0.0).astype(jnp.bfloat16)
        writes[index].start()
    for write in writes:
        write.wait()


def attend_local(queries, received, length, head_dim, after):
    seq_len, width = queries.shape
    heads = width // head_dim
    return pl.pallas_call(
        functools.partial(attend_kernel, heads=heads),
        in_specs=[SMEM, ANYWHERE, VMEM, ANYWHERE],
        out_specs=ANYWHERE,
        out_shape=jax.ShapeDtypeStruct((seq_len, width), jnp.bfloat16),
        scratch_shapes=[
            pltpu.VMEM((seq_len, width), jnp.bfloat16),
            pltpu.VMEM((seq_len, width), jnp.bfloat16),
            pltpu.SemaphoreType.DMA((2, seq_len // BLOCK)),
            pltpu.VMEM((seq_len, head_dim), jnp.bfloat16),
            pltpu.VMEM((seq_len, 2 * head_dim), jnp.bfloat16),
        ],
        compiler_params=pltpu.CompilerParams(vmem_limit_bytes=62 * 1024 * 1024),
        cost_estimate=pl.CostEstimate(
            flops=4 * seq_len * seq_len * width,
            bytes_accessed=4 * seq_len * width,
            transcendentals=seq_len * seq_len * heads,
        ),
        name="attend",
    )(length, queries, received, after)


def placeholder(shape):
    def nothing(out_ref):
        del out_ref

    return pl.pallas_call(
        nothing,
        out_specs=pl.BlockSpec(memory_space=pl.ANY),
        out_shape=jax.ShapeDtypeStruct(shape, jnp.bfloat16),
        name="placeholder",
    )()


def butterflies(values):
    values = list(values)
    stride = 1
    while stride < len(values):
        for low in range(len(values)):
            if not low & stride:
                a, b = values[low], values[low + stride]
                values[low], values[low + stride] = a + b, a - b
        stride *= 2
    return values


def hadamard_kernel(in_ref, after_ref, out_ref, mid_ref, *, heads):
    del after_ref
    devices, tokens, width = in_ref.shape
    head_dim = width // heads
    factor = 1.0 / math.sqrt(devices * heads)
    columns = [slice(h * head_dim, (h + 1) * head_dim) for h in range(heads)]
    for first in range(0, tokens, PAGE):
        rows = slice(first, first + PAGE)
        for device in range(devices):
            tiles = butterflies([in_ref[device, rows, c].astype(jnp.float32) for c in columns])
            for c, tile in zip(columns, tiles):
                mid_ref[device, :, c] = tile
        for c in columns:
            tiles = butterflies([mid_ref[device, :, c] for device in range(devices)])
            for device, tile in enumerate(tiles):
                out_ref[device, rows, c] = (tile * factor).astype(jnp.bfloat16)


def hadamard(blocks, heads, after):
    devices, tokens, width = blocks.shape
    spec = pl.BlockSpec((devices, PAGE, width), lambda i: (0, i, 0))
    return pl.pallas_call(
        functools.partial(hadamard_kernel, heads=heads),
        grid=(tokens // PAGE,),
        in_specs=[spec, pl.BlockSpec(memory_space=pl.ANY)],
        out_specs=spec,
        out_shape=jax.ShapeDtypeStruct(blocks.shape, jnp.bfloat16),
        scratch_shapes=[pltpu.VMEM((devices, PAGE, width), jnp.float32)],
        compiler_params=pltpu.CompilerParams(vmem_limit_bytes=32 * 1024 * 1024),
        cost_estimate=pl.CostEstimate(
            flops=7 * blocks.size, bytes_accessed=4 * blocks.size, transcendentals=0
        ),
        name="hadamard",
    )(blocks, after)


def page_kernel(
    length_ref, level_ref, side_ref, owner_ref, kv_ref, out_ref, count_ref, slot_ref, *, capacity
):
    sources, _, tokens, head_dim = kv_ref.shape
    owners = out_ref.shape[0]
    per_source = tokens // PAGE
    out_ref[...] = jnp.zeros_like(out_ref)
    level = level_ref[0].astype(jnp.float32)
    side = side_ref[0]
    rows = lax.broadcasted_iota(jnp.int32, (PAGE, head_dim), 0)
    tail = lax.broadcasted_iota(jnp.int32, (PAGE, head_dim), 0)
    for owner in range(owners):
        count_ref[owner] = 0
    for page in range(sources * per_source):
        owner = owner_ref[page]
        slot_ref[page] = jnp.minimum(count_ref[owner], capacity - 1)
        count_ref[owner] = count_ref[owner] + 1

    for page in range(sources * per_source):
        part = page % per_source
        values = kv_ref[page // per_source, side, part * PAGE : (part + 1) * PAGE, :]
        values = jnp.where(page * PAGE + rows < length_ref[0], values.astype(jnp.float32), 0.0)
        total = jnp.sum(values * values, axis=(0, 1), keepdims=True)
        rms = jnp.sqrt(total / (PAGE * head_dim) + 1e-06)
        step = (rms * 0.5).astype(jnp.bfloat16).astype(jnp.float32)
        codes = jnp.clip(values / step, -level, level).astype(jnp.bfloat16)
        owner = owner_ref[page]
        slot = slot_ref[page]
        out_ref[owner, pl.ds(pl.multiple_of(slot * PAGE, PAGE), PAGE), :] = codes
        before = out_ref[owner, capacity * PAGE :, :].astype(jnp.float32)
        steps = jnp.where(tail == slot, jnp.broadcast_to(step, tail.shape), before)
        out_ref[owner, capacity * PAGE :, :] = steps.astype(jnp.bfloat16)


def page_table(received, length, level, owner_of, owners, capacity):
    head_dim = received.shape[3]
    smem = pl.BlockSpec(memory_space=pltpu.SMEM)
    vmem = pl.BlockSpec(memory_space=pltpu.VMEM)
    side = (lax.axis_index("tp") % 2).astype(jnp.int32).reshape(1)
    shape = (owners, (capacity + 1) * PAGE, head_dim)
    return pl.pallas_call(
        functools.partial(page_kernel, capacity=capacity),
        in_specs=[smem, smem, smem, smem, vmem],
        out_specs=vmem,
        out_shape=jax.ShapeDtypeStruct(shape, jnp.bfloat16),
        scratch_shapes=[
            pltpu.SMEM((owners,), jnp.int32),
            pltpu.SMEM(owner_of.shape, jnp.int32),
        ],
        compiler_params=pltpu.CompilerParams(vmem_limit_bytes=32 * 1024 * 1024),
        cost_estimate=pl.CostEstimate(
            flops=10 * received.size, bytes_accessed=2 * received.size, transcendentals=0
        ),
        name="pages",
    )(length, level, side, owner_of, received)


def to_owners(table, axis, bits, members):
    count = lax.axis_size(axis)
    position = lax.axis_index(axis)
    inner = table.shape[1:]
    for bit in bits:
        stride = 1 << bit
        upper = jnp.right_shift(position, bit) % 2
        halves = table.reshape((count // (2 * stride), 2, stride) + inner)
        keep = lax.dynamic_index_in_dim(halves, upper, 1, keepdims=False)
        send = lax.dynamic_index_in_dim(halves, 1 - upper, 1, keepdims=False)
        got = lax.ppermute(send, axis, [(i, i ^ stride) for i in members])
        low = jnp.where(upper == 0, keep, got)
        high = jnp.where(upper == 0, got, keep)
        table = jnp.stack([low, high], axis=1).reshape((count,) + inner)
    return table


def body(queries, kv_heads, bit_widths, destinations, lengths):
    local_kv = kv_heads[0]
    total_rows, tok_here, head_dim = local_kv.shape
    tp_count = lax.axis_size("tp")
    owners = lax.axis_size("req")
    paired = local_kv.reshape(total_rows // 2, 2, tok_here, head_dim)
    outgoing = jnp.repeat(paired, tp_count // (total_rows // 2), axis=0)
    received = lax.all_to_all(outgoing, "tp", split_axis=0, concat_axis=0, tiled=True)
    seq_len = tp_count * tok_here
    heads_here = queries.shape[2] // head_dim

    pages = seq_len // PAGE
    capacity = max(2, (3 * pages + 2 * owners - 1) // (2 * owners))
    level = 2 ** (bit_widths - 1) - 1
    bits = list(range(1, owners.bit_length() - 1)) + [0]
    first_bits, last_bits = bits[:EARLY], bits[EARLY:]
    odd = lax.axis_index("req") % 2 == 1

    def start_pages(members):
        table = page_table(received, lengths, level, destinations[0, :, 0], owners, capacity)
        return to_owners(table, "req", first_bits, members)

    shape = (owners, (capacity + 1) * PAGE, head_dim)
    table = lax.cond(
        odd,
        lambda: start_pages(range(1, owners, 2)),
        lambda: placeholder(shape),
    )
    attended = attend_local(queries[0], received, lengths, head_dim, table)
    blocks = attended.reshape(tp_count, seq_len // tp_count, heads_here * head_dim)
    blocks = lax.all_to_all(blocks, "tp", split_axis=0, concat_axis=0, tiled=True)
    table = lax.cond(odd, lambda t: t, lambda t: start_pages(range(0, owners, 2)), table)
    mixed = hadamard(blocks, heads_here, table)
    back = lax.all_to_all(mixed, "tp", split_axis=0, concat_axis=0, tiled=True)
    rotated = back.reshape(1, seq_len, heads_here * head_dim)
    table = to_owners(table, "req", last_bits, range(owners))
    got_codes = table[:, : capacity * PAGE].reshape(1, owners, capacity, 1, PAGE, head_dim)
    got_steps = table[:, capacity * PAGE : capacity * (PAGE + 1), 0]
    return rotated, got_codes, got_steps.reshape(1, owners, capacity, 1)


def solution(mesh):
    in_specs = (
        P("req", None, "tp"),
        P("req", None, "tp", None),
        P("tp"),
        P("req", None, None),
        P("req"),
    )
    out_specs = (
        P("req", None, "tp"),
        P("req", None, None, "tp", None, None),
        P("req", None, None, "tp"),
    )
    return jax.shard_map(body, mesh=mesh, in_specs=in_specs, out_specs=out_specs, check_vma=False)
```

```python
import functools
import math

import jax
import jax.numpy as jnp
from jax import lax
from jax.experimental import pallas as pl
from jax.experimental.pallas import tpu as pltpu
from jax.sharding import PartitionSpec as P

PAGE = 16
EARLY = 3
SMEM = pl.BlockSpec(memory_space=pltpu.SMEM)
VMEM = pl.BlockSpec(memory_space=pltpu.VMEM)
ANYWHERE = pl.BlockSpec(memory_space=pl.ANY)
BLOCK = 256


def attend_kernel(
    length_ref, q_hbm, kv_ref, after_ref, out_hbm, q_ref, out_ref, sems, k_ref, v_ref, *, heads
):
    del after_ref
    seq_len, head_dim = k_ref.shape
    parts = [slice(first, first + BLOCK) for first in range(0, seq_len, BLOCK)]
    fetches = [
        pltpu.make_async_copy(q_hbm.at[part], q_ref.at[part], sems.at[0, index])
        for index, part in enumerate(parts)
    ]
    writes = [
        pltpu.make_async_copy(out_ref.at[part], out_hbm.at[part], sems.at[1, index])
        for index, part in enumerate(parts)
    ]
    for fetch in fetches:
        fetch.start()
    k_ref[...] = kv_ref[:, 0].reshape(seq_len, head_dim)
    v_ref[:, :head_dim] = kv_ref[:, 1].reshape(seq_len, head_dim)
    v_ref[:, head_dim:] = jnp.ones((seq_len, head_dim), jnp.bfloat16)
    rate = math.log2(math.e) / math.sqrt(head_dim)
    rows = lax.broadcasted_iota(jnp.int32, (BLOCK, BLOCK), 0)
    cols = lax.broadcasted_iota(jnp.int32, (BLOCK, BLOCK), 1)
    causal = rows >= cols
    row = lax.broadcasted_iota(jnp.int32, (BLOCK, head_dim), 0)

    for index, part in enumerate(parts):
        fetches[index].wait()
        start, finish = part.start, part.stop
        live = row + start < length_ref[0]
        for column in range(0, heads * head_dim, head_dim):
            columns = slice(column, column + head_dim)
            scores = lax.dot_general(
                q_ref[part, columns],
                k_ref[:finish],
                (((1,), (1,)), ((), ())),
                preferred_element_type=jnp.float32,
            )
            last = jnp.where(causal, scores[:, start:], -jnp.inf)
            scores = jnp.concatenate([scores[:, :start], last], axis=1) if start else last
            top = jnp.max(scores, axis=1, keepdims=True)
            weights = jnp.exp2((scores - top) * rate).astype(jnp.bfloat16)
            both = jnp.dot(weights, v_ref[:finish], preferred_element_type=jnp.float32)
            attended = both[:, :head_dim] / both[:, head_dim:]
            out_ref[part, columns] = jnp.where(live, attended, 0.0).astype(jnp.bfloat16)
        writes[index].start()
    for write in writes:
        write.wait()


def attend_local(queries, received, length, head_dim, after):
    seq_len, width = queries.shape
    heads = width // head_dim
    return pl.pallas_call(
        functools.partial(attend_kernel, heads=heads),
        in_specs=[SMEM, ANYWHERE, VMEM, ANYWHERE],
        out_specs=ANYWHERE,
        out_shape=jax.ShapeDtypeStruct((seq_len, width), jnp.bfloat16),
        scratch_shapes=[
            pltpu.VMEM((seq_len, width), jnp.bfloat16),
            pltpu.VMEM((seq_len, width), jnp.bfloat16),
            pltpu.SemaphoreType.DMA((2, seq_len // BLOCK)),
            pltpu.VMEM((seq_len, head_dim), jnp.bfloat16),
            pltpu.VMEM((seq_len, 2 * head_dim), jnp.bfloat16),
        ],
        compiler_params=pltpu.CompilerParams(vmem_limit_bytes=62 * 1024 * 1024),
        cost_estimate=pl.CostEstimate(
            flops=4 * seq_len * seq_len * width,
            bytes_accessed=4 * seq_len * width,
            transcendentals=seq_len * seq_len * heads,
        ),
        name="attend",
    )(length, queries, received, after)


def placeholder(shape):
    def nothing(out_ref):
        del out_ref

    return pl.pallas_call(
        nothing,
        out_specs=pl.BlockSpec(memory_space=pl.ANY),
        out_shape=jax.ShapeDtypeStruct(shape, jnp.bfloat16),
        name="placeholder",
    )()


def butterflies(values):
    values = list(values)
    stride = 1
    while stride < len(values):
        for low in range(len(values)):
            if not low & stride:
                a, b = values[low], values[low + stride]
                values[low], values[low + stride] = a + b, a - b
        stride *= 2
    return values


def hadamard_kernel(in_ref, after_ref, out_ref, mid_ref, *, heads):
    del after_ref
    devices, tokens, width = in_ref.shape
    head_dim = width // heads
    factor = 1.0 / math.sqrt(devices * heads)
    columns = [slice(h * head_dim, (h + 1) * head_dim) for h in range(heads)]
    for first in range(0, tokens, PAGE):
        rows = slice(first, first + PAGE)
        for device in range(devices):
            tiles = butterflies([in_ref[device, rows, c].astype(jnp.float32) for c in columns])
            for c, tile in zip(columns, tiles):
                mid_ref[device, :, c] = tile
        for c in columns:
            tiles = butterflies([mid_ref[device, :, c] for device in range(devices)])
            for device, tile in enumerate(tiles):
                out_ref[device, rows, c] = (tile * factor).astype(jnp.bfloat16)


def hadamard(blocks, heads, after):
    devices, _, width = blocks.shape
    return pl.pallas_call(
        functools.partial(hadamard_kernel, heads=heads),
        in_specs=[VMEM, ANYWHERE],
        out_specs=VMEM,
        out_shape=jax.ShapeDtypeStruct(blocks.shape, jnp.bfloat16),
        scratch_shapes=[pltpu.VMEM((devices, PAGE, width), jnp.float32)],
        compiler_params=pltpu.CompilerParams(vmem_limit_bytes=32 * 1024 * 1024),
        cost_estimate=pl.CostEstimate(
            flops=7 * blocks.size, bytes_accessed=4 * blocks.size, transcendentals=0
        ),
        name="hadamard",
    )(blocks, after)


def page_kernel(
    length_ref, level_ref, side_ref, owner_ref, kv_ref, out_ref, count_ref, slot_ref, *, capacity
):
    sources, _, tokens, head_dim = kv_ref.shape
    owners = out_ref.shape[0]
    per_source = tokens // PAGE
    out_ref[...] = jnp.zeros_like(out_ref)
    level = level_ref[0].astype(jnp.float32)
    side = side_ref[0]
    rows = lax.broadcasted_iota(jnp.int32, (PAGE, head_dim), 0)
    tail = lax.broadcasted_iota(jnp.int32, (PAGE, head_dim), 0)
    for owner in range(owners):
        count_ref[owner] = 0
    for page in range(sources * per_source):
        owner = owner_ref[page]
        slot_ref[page] = jnp.minimum(count_ref[owner], capacity - 1)
        count_ref[owner] = count_ref[owner] + 1

    for page in range(sources * per_source):
        part = page % per_source
        values = kv_ref[page // per_source, side, part * PAGE : (part + 1) * PAGE, :]
        values = jnp.where(page * PAGE + rows < length_ref[0], values.astype(jnp.float32), 0.0)
        total = jnp.sum(values * values, axis=(0, 1), keepdims=True)
        rms = jnp.sqrt(total / (PAGE * head_dim) + 1e-06)
        step = (rms * 0.5).astype(jnp.bfloat16).astype(jnp.float32)
        codes = jnp.clip(values / step, -level, level).astype(jnp.bfloat16)
        owner = owner_ref[page]
        slot = slot_ref[page]
        out_ref[owner, pl.ds(pl.multiple_of(slot * PAGE, PAGE), PAGE), :] = codes
        before = out_ref[owner, capacity * PAGE :, :].astype(jnp.float32)
        steps = jnp.where(tail == slot, jnp.broadcast_to(step, tail.shape), before)
        out_ref[owner, capacity * PAGE :, :] = steps.astype(jnp.bfloat16)


def page_table(received, length, level, owner_of, owners, capacity):
    head_dim = received.shape[3]
    smem = pl.BlockSpec(memory_space=pltpu.SMEM)
    vmem = pl.BlockSpec(memory_space=pltpu.VMEM)
    side = (lax.axis_index("tp") % 2).astype(jnp.int32).reshape(1)
    shape = (owners, (capacity + 1) * PAGE, head_dim)
    return pl.pallas_call(
        functools.partial(page_kernel, capacity=capacity),
        in_specs=[smem, smem, smem, smem, vmem],
        out_specs=vmem,
        out_shape=jax.ShapeDtypeStruct(shape, jnp.bfloat16),
        scratch_shapes=[
            pltpu.SMEM((owners,), jnp.int32),
            pltpu.SMEM(owner_of.shape, jnp.int32),
        ],
        compiler_params=pltpu.CompilerParams(vmem_limit_bytes=32 * 1024 * 1024),
        cost_estimate=pl.CostEstimate(
            flops=10 * received.size, bytes_accessed=2 * received.size, transcendentals=0
        ),
        name="pages",
    )(length, level, side, owner_of, received)


def to_owners(table, axis, bits, members):
    count = lax.axis_size(axis)
    position = lax.axis_index(axis)
    inner = table.shape[1:]
    for bit in bits:
        stride = 1 << bit
        upper = jnp.right_shift(position, bit) % 2
        halves = table.reshape((count // (2 * stride), 2, stride) + inner)
        keep = lax.dynamic_index_in_dim(halves, upper, 1, keepdims=False)
        send = lax.dynamic_index_in_dim(halves, 1 - upper, 1, keepdims=False)
        got = lax.ppermute(send, axis, [(i, i ^ stride) for i in members])
        low = jnp.where(upper == 0, keep, got)
        high = jnp.where(upper == 0, got, keep)
        table = jnp.stack([low, high], axis=1).reshape((count,) + inner)
    return table


def body(queries, kv_heads, bit_widths, destinations, lengths):
    local_kv = kv_heads[0]
    total_rows, tok_here, head_dim = local_kv.shape
    tp_count = lax.axis_size("tp")
    owners = lax.axis_size("req")
    paired = local_kv.reshape(total_rows // 2, 2, tok_here, head_dim)
    outgoing = jnp.repeat(paired, tp_count // (total_rows // 2), axis=0)
    received = lax.all_to_all(outgoing, "tp", split_axis=0, concat_axis=0, tiled=True)
    seq_len = tp_count * tok_here
    heads_here = queries.shape[2] // head_dim

    pages = seq_len // PAGE
    capacity = max(2, (3 * pages + 2 * owners - 1) // (2 * owners))
    level = 2 ** (bit_widths - 1) - 1
    bits = list(range(1, owners.bit_length() - 1)) + [0]
    first_bits, last_bits = bits[:EARLY], bits[EARLY:]
    odd = lax.axis_index("req") % 2 == 1

    def start_pages(members):
        table = page_table(received, lengths, level, destinations[0, :, 0], owners, capacity)
        return to_owners(table, "req", first_bits, members)

    shape = (owners, (capacity + 1) * PAGE, head_dim)
    table = lax.cond(
        odd,
        lambda: start_pages(range(1, owners, 2)),
        lambda: placeholder(shape),
    )
    attended = attend_local(queries[0], received, lengths, head_dim, table)
    blocks = attended.reshape(tp_count, seq_len // tp_count, heads_here * head_dim)
    blocks = lax.all_to_all(blocks, "tp", split_axis=0, concat_axis=0, tiled=True)
    table = lax.cond(odd, lambda t: t, lambda t: start_pages(range(0, owners, 2)), table)
    mixed = hadamard(blocks, heads_here, table)
    back = lax.all_to_all(mixed, "tp", split_axis=0, concat_axis=0, tiled=True)
    rotated = back.reshape(1, seq_len, heads_here * head_dim)
    table = to_owners(table, "req", last_bits, range(owners))
    got_codes = table[:, : capacity * PAGE].reshape(1, owners, capacity, 1, PAGE, head_dim)
    got_steps = table[:, capacity * PAGE : capacity * (PAGE + 1), 0]
    return rotated, got_codes, got_steps.reshape(1, owners, capacity, 1)


def solution(mesh):
    in_specs = (
        P("req", None, "tp"),
        P("req", None, "tp", None),
        P("tp"),
        P("req", None, None),
        P("req"),
    )
    out_specs = (
        P("req", None, "tp"),
        P("req", None, None, "tp", None, None),
        P("req", None, None, "tp"),
    )
    return jax.shard_map(body, mesh=mesh, in_specs=in_specs, out_specs=out_specs, check_vma=False)
```
